256 devices in a mesh: replica: 16 (over y_lo, x, core), fsdp: 16 (over z, y_hi).
Axes of the slice: x: 4, y: 4 (y_hi: 2, y_lo: 2; y = y_hi * 2 + y_lo), z: 8, core: 2. Of those that a mesh axis runs over, the one named last changes fastest.
Arguments:
- tokens: bfloat16 [65536, 8192], P(('replica', 'fsdp')), may hold values from -300 to 300
- norm_gain: float32 [16, 8192], P('replica'), may hold values from 0.5 to 1.5
- cotangent: bfloat16 [65536, 512], P(('replica', 'fsdp')), may hold values from -0.09375 to 0.09375
- value_weight: bfloat16 [16, 8192, 512], P('replica', 'fsdp'), may hold values from -0.03125 to 0.03125
- first_moment: float32 [16, 8192, 512], P('replica', 'fsdp'), may hold values from -3 to 3
- second_moment: float32 [16, 8192, 512], P('replica', 'fsdp'), may hold values from 0.1 to 2
- pseudo_grad: bfloat16 [16, 8192, 1024], P('replica', 'fsdp'), may hold values from -6 to 6
- fragment: float32 [8192, 1024], P(('fsdp', 'replica')), may hold values from -0.3 to 0.3
- outer_momentum: float32 [8192, 1024], P(('fsdp', 'replica')), may hold values from -3 to 3
Outputs:
- values: bfloat16 [65536, 512], P(('replica', 'fsdp'))
- new_value_weight: bfloat16 [16, 8192, 512], P('replica', 'fsdp')
- new_first: float32 [16, 8192, 512], P('replica', 'fsdp')
- new_second: float32 [16, 8192, 512], P('replica', 'fsdp')
- new_fragment: bfloat16 [8192, 1024], P('fsdp')
- new_outer_momentum: float32 [8192, 1024], P(('fsdp', 'replica'))
The draws below stay inside these ranges and needn't reach their ends.
All inputs are finite; a program needn't handle non-finite values.
Results may differ from the reference program's by a relative error of at most 0.019.
Values may be sent and summed in bfloat16 or wider, within the bound.
No kernel may reach another device: no remote copies, remote signals or barrier semaphores. Data moves between devices by JAX's collectives and lax.ppermute only.
A program may use at most 128 MiB of HBM per device.

```python
import math
import jax
import jax.numpy as jnp
from jax import lax

D = 8192
KD = 1024
KVW = 512
TOK_DEV = 256
TOKENS = 65536
N_REPLICA = 16
N_FSDP = 16


def draw_tokens(key, part):
    key = jax.random.fold_in(key, 11)
    key_base, key_cols, key_rows = jax.random.split(key, 3)
    column_scale = jnp.exp(jax.random.uniform(key_cols, (1, D), jnp.float32) * 2.302585)
    row_scale = jnp.exp(jax.random.uniform(key_rows, (TOKENS, 1), jnp.float32) * 2.302585)
    base = jnp.clip(jax.random.normal(key_base, (TOKENS, D), jnp.float32), -3.0, 3.0)
    return (0.3 * base * column_scale * row_scale).astype(jnp.bfloat16)


def levels(own_key, dims, pieces, low, top_value):
    level = 1.0
    for position, blocks in pieces:
        draws = jax.random.uniform(jax.random.fold_in(jax.random.fold_in(own_key, 6), position), (blocks,), jnp.float32, low / len(pieces), top_value / len(pieces))
        level = level * jnp.repeat(jnp.exp(draws), dims[position] // blocks).reshape((-1,) + (1,) * (len(dims) - 1 - position))
    return level


def centred(key, dims, width, limit, shards=(), held_as=jnp.bfloat16):
    entries = width * jax.random.normal(key, dims, jnp.float32)
    if shards:
        entries = entries * levels(key, dims, shards, -0.22, 0.18)
    return jnp.clip(entries, -limit, limit).astype(held_as)


def setup_inputs(seed: int = 0) -> dict:
    arg_keys = jax.random.split(jax.random.key(seed), 10)
    tokens = draw_tokens(jax.random.fold_in(arg_keys[9], 71), 0)
    norm_gain = jnp.clip(1.0 + 0.1 * jax.random.normal(arg_keys[1], (N_REPLICA, D), jnp.float32), 0.5, 1.5)
    cotangent = centred(arg_keys[2], (TOKENS, KVW), ((TOK_DEV * N_FSDP) ** -0.5), 0.09375, ((0, 256),))
    value_weight = centred(arg_keys[3], (N_REPLICA, D, KVW), (4 * D) ** -0.5, 0.03125, ((0, 16), (1, 16)))
    first_moment = centred(arg_keys[4], (N_REPLICA, D, KVW), 0.5, 3.0, ((0, 16), (1, 16)), jnp.float32)
    second_moment = jnp.clip(jnp.exp(math.log(2.0) - 2.9957323 * jax.random.uniform(arg_keys[5], (N_REPLICA, D, KVW), jnp.float32) ** levels(arg_keys[5], (N_REPLICA, D, KVW), ((0, 16), (1, 16)), -0.2, 0.2)), 0.1, 2.0)
    pseudo_grad = centred(arg_keys[6], (N_REPLICA, D, KD), 1.0, 6.0, ((0, 16), (1, 16)))
    fragment = centred(arg_keys[7], (D, KD), 0.05, 0.3, ((0, 256),), jnp.float32)
    outer_momentum = centred(arg_keys[8], (D, KD), 0.5, 3.0, ((0, 256),), jnp.float32)
    return {"tokens": tokens, "norm_gain": norm_gain, "cotangent": cotangent, "value_weight": value_weight, "first_moment": first_moment, "second_moment": second_moment, "pseudo_grad": pseudo_grad, "fragment": fragment, "outer_momentum": outer_momentum}


def inner_step(args):
    rows, gain, cot, weight, first, second = args
    wide = rows.astype(jnp.float32)
    inverse_rms = lax.rsqrt(lax.optimization_barrier(jnp.mean(wide * wide, axis=-1, keepdims=True)) + 1e-05)
    normed = (wide * inverse_rms * gain[None, :]).astype(jnp.bfloat16)
    values = jnp.dot(normed, weight, preferred_element_type=jnp.float32).astype(jnp.bfloat16)
    gradient = jnp.dot(normed.T, cot, preferred_element_type=jnp.float32)
    new_first = 0.9 * first + 0.1 * gradient
    new_second = 0.95 * second + 0.05 * gradient * gradient
    update = new_first / 0.6513215599 / (jnp.sqrt(new_second / 0.4012630607) + 1e-08)
    update = update + 0.1 * weight.astype(jnp.float32)
    new_weight = (weight.astype(jnp.float32) - 0.003 * update).astype(jnp.bfloat16)
    return (values, new_weight, new_first, new_second)

def reference(tokens, norm_gain, cotangent, value_weight, first_moment, second_moment, pseudo_grad, fragment, outer_momentum):
    rows = tokens.reshape(N_REPLICA, TOK_DEV * N_FSDP, D)
    cots = cotangent.reshape(N_REPLICA, TOK_DEV * N_FSDP, KVW)
    values, new_weight, new_first, new_second = lax.map(inner_step, (rows, norm_gain, cots, value_weight, first_moment, second_moment))
    values = values.reshape(TOKENS, KVW)
    average = lax.optimization_barrier(jnp.sum(pseudo_grad.astype(jnp.float32), axis=0)) / N_REPLICA
    new_momentum = 0.9 * outer_momentum + average
    new_fragment = (fragment - 0.7 * (average + 0.9 * new_momentum)).astype(jnp.bfloat16)
    return (values, new_weight, new_first, new_second, new_fragment, new_momentum)
```

```python
import jax
import jax.numpy as jnp
from jax import lax
from jax.experimental import pallas as pl
from jax.experimental.pallas import tpu as pltpu
from jax.sharding import Mesh, PartitionSpec as P

F32 = jnp.float32
BF16 = jnp.bfloat16
CORES, RING, COLUMN = 2, 8, 4
AROUND = [(z, (z + 1) % RING) for z in range(RING)] + [
    (RING + z, RING + (z - 1) % RING) for z in range(RING)
]
NEXT = [(0, 1), (1, 0), (2, 3), (3, 2)]
OUTER = [(0, 3), (3, 0), (1, 2), (2, 1)]
SWAP = [(0, 1), (1, 0)]
HINT = pl.CostEstimate(flops=4_000_000_000, bytes_accessed=20_000_000, transcendentals=0)
BRIEF = pl.CostEstimate(flops=1000, bytes_accessed=1000, transcendentals=0)


def around(value):
    return lax.ppermute(value, ("c", "z"), AROUND)


def matmul(left, right):
    return lax.dot_general(left, right, (((1,), (0,)), ((), ())), preferred_element_type=F32)


def contract_rows(left, right):
    return lax.dot_general(left, right, (((0,), (0,)), ((), ())), preferred_element_type=F32)


def whole(shape):
    return pl.BlockSpec(shape, lambda i, *_: (0,) * len(shape))


def lead(place, array):
    return pl.BlockSpec((1,) + array.shape[1:], lambda i, *_: (place,) + (0,) * (array.ndim - 1))


def tiled(shape, axis, tile):
    block = shape[:axis] + (tile,) + shape[axis + 1 :]
    return pl.BlockSpec(block, lambda i, *_: tuple(i if d == axis else 0 for d in range(len(shape))))


def turn(kernel, inputs, outs, scalars=None, steps=1, after=(), hint=HINT):
    arrays, specs = [a for a, _ in inputs], [s for _, s in inputs]
    for array in after:
        arrays.append(array)
        specs.append(whole((1,) * (array.ndim - 2) + (16, 128)))
    many = len(inputs)
    prefetched = [] if scalars is None else [jnp.stack([jnp.int32(s) for s in scalars])]

    def run(*refs):
        first = len(prefetched)
        ins, rest = refs[first : first + many], refs[first + len(arrays) :]
        kernel(refs[0] if prefetched else None, ins, rest)

    return pl.pallas_call(
        run,
        grid_spec=pltpu.PrefetchScalarGridSpec(
            num_scalar_prefetch=len(prefetched),
            grid=(steps,),
            in_specs=specs,
            out_specs=[s for _, s in outs],
        ),
        out_shape=[o for o, _ in outs],
        compiler_params=pltpu.CompilerParams(vmem_limit_bytes=16 * 2**20),
        cost_estimate=hint,
    )(*prefetched, *arrays)


def full(array):
    return array, whole(array.shape)


def new(shape, dtype):
    return jax.ShapeDtypeStruct(shape, dtype), whole(shape)


def far(array, blocks):
    return pltpu.with_memory_space_constraint(array, pltpu.HBM), blocks


def scaled(tokens_ref, gain_ref, inverse_rms, start, depth):
    at = pl.ds(pl.multiple_of(start, depth), depth)
    return (tokens_ref[:, at].astype(F32) * inverse_rms * gain_ref[:, at]).astype(BF16)


def first_block(start, tokens, norm_gain, depth):
    rows, width = tokens.shape
    tile = rows // 4

    def kernel(starts, ins, outs):
        tokens_ref, gain_ref = ins
        wide = tokens_ref[...].astype(F32)
        inverse_rms = lax.rsqrt(jnp.mean(wide * wide, axis=-1, keepdims=True) + 1e-05)
        outs[0][0] = scaled(tokens_ref, gain_ref, inverse_rms, starts[0], depth)
        outs[1][...] = jnp.broadcast_to(inverse_rms, outs[1].shape)

    block, inverse = (1, rows, depth), (rows, 128)
    return turn(
        kernel,
        [(tokens, tiled(tokens.shape, 0, tile)), full(norm_gain)],
        [
            (jax.ShapeDtypeStruct(block, BF16), tiled(block, 1, tile)),
            (jax.ShapeDtypeStruct(inverse, F32), tiled(inverse, 0, tile)),
        ],
        [start],
        4,
        hint=BRIEF,
    )


def normed_blocks(starts, sizes, tokens, norm_gain, inverse, depth, after=()):
    rows, width = tokens.shape
    tile = rows // 4

    def kernel(starts, ins, outs):
        tokens_ref, gain_ref, inverse_ref = ins
        at = 0
        for out, size in zip(outs, sizes):
            for place in range(size):
                out[place] = scaled(tokens_ref, gain_ref, inverse_ref[:, :1], starts[at], depth)
                at += 1

    shapes = [(size, rows, depth) for size in sizes]
    return turn(
        kernel,
        [
            (tokens, tiled(tokens.shape, 0, tile)),
            full(norm_gain),
            (inverse, tiled(inverse.shape, 0, tile)),
        ],
        [(pltpu.HBM(shape, BF16), tiled(shape, 1, tile)) for shape in shapes],
        starts,
        4,
        after,
    )


def copied(array, after):
    def kernel(_, ins, outs):
        outs[0][...] = ins[0][...]

    return turn(kernel, [full(array)], [new(array.shape, array.dtype)], after=after)[0]


def gradient_step(mine, theirs, cotangents, arrived, dtype, after=()):
    depth, columns = mine[0].shape[-1], cotangents[0].shape[1]
    inputs = [far(*mine), far(*theirs)] + [full(c) for c in cotangents]
    inputs += [] if arrived is None else [full(arrived)]

    def kernel(_, ins, outs):
        total = contract_rows(ins[0][0], ins[2][...]) + contract_rows(ins[1][0], ins[3][...])
        if arrived is not None:
            total = total + ins[4][...].astype(F32)
        outs[0][...] = total.astype(dtype)

    return turn(kernel, inputs, [new((depth, columns), dtype)], after=after)[0]


def value_step(mine, theirs, weights, sums, last=False, after=()):
    many = len(weights)
    rows, columns = mine[0][0].shape[1], weights[0].shape[1]
    inputs = [far(*m) for m in mine] + [far(*t) for t in theirs] + [full(w) for w in weights] + [full(s) for s in sums]

    def kernel(_, ins, outs):
        for side in range(2):
            value = sum(matmul(ins[side * many + p][0], ins[2 * many + p][...]) for p in range(many))
            if sums:
                value = value + ins[3 * many + side][...]
            outs[side][...] = value.astype(outs[side].dtype)

    shape = (rows, columns)
    return turn(kernel, inputs, [new(shape, F32), new(shape, BF16 if last else F32)], after=after)


def rows_of_core(parts, core, after):
    lines, columns, _, rows, width = parts.shape

    def kernel(_, ins, outs):
        outs[0][...] = ins[0][:, :, 0].swapaxes(0, 1)

    block = pl.BlockSpec((lines, columns, 1, rows, width), lambda i, core: (0, 0, core[0], 0, 0))
    return turn(kernel, [(parts, block)], [new((columns, lines, rows, width), BF16)], [core], 1, after, BRIEF)[0]


def sum_and_split(mine, got, picks, core=None, first=BF16, after=()):
    shape = got.shape
    sizes = [len(group) for group in picks]
    places = [p for group in picks for p in group]
    spec = whole(mine.shape)
    if core is not None:
        lines, columns, _, rows, width = mine.shape
        last = len(places)
        places.append(core)
        spec = pl.BlockSpec((lines, columns, 1, rows, width), lambda i, s: (0, 0, s[last], 0, 0))

    def kernel(places, ins, outs):
        at = 0
        for out, size in zip(outs, sizes):
            for place in range(size):
                index = places[at]
                held = ins[0][index] if core is None else ins[0][:, index, 0]
                out[place] = (held.astype(F32) + ins[1][index].astype(F32)).astype(out.dtype)
                at += 1

    outs = [new((size,) + shape[1:], first if out == 0 else BF16) for out, size in enumerate(sizes)]
    return turn(kernel, [(mine, spec), full(got)], outs, places, 1, after)


def outer_step(mine, got, fragment, momentum, after):
    def kernel(_, ins, outs):
        average = (ins[0][0] + ins[1][0].astype(F32)) / 16
        moved = 0.9 * ins[3][...] + average
        outs[0][0] = (ins[2][...] - 0.7 * (average + 0.9 * moved)).astype(BF16)
        outs[1][...] = moved

    shape = fragment.shape
    return turn(
        kernel,
        [full(mine), full(got), full(fragment), full(momentum)],
        [new((1,) + shape, BF16), new(shape, F32)],
        after=after,
    )


def join(mine, got, places, after=()):
    many = mine.shape[0]

    def kernel(places, ins, outs):
        for side in range(2):
            for place in range(many):
                outs[0][places[side * many + place]] = ins[side][place]

    return turn(kernel, [full(mine), full(got)], [new((2 * many,) + mine.shape[1:], BF16)], places, 1, after)[0]


def join_cores(core, mine, got):
    columns, lines, rows, width = mine.shape

    def kernel(core, ins, outs):
        for line in range(lines):
            for column in range(columns):
                outs[0][line, column, core[0]] = ins[0][column, line]
                outs[0][line, column, 1 - core[0]] = ins[1][column, line]

    return turn(kernel, [full(mine), full(got)], [new((lines, columns, CORES, rows, width), BF16)], [core])[0]


def body(
    tokens,
    norm_gain,
    cotangent,
    value_weight,
    first_moment,
    second_moment,
    pseudo_grad,
    fragment,
    outer_momentum,
):
    x, core, row = lax.axis_index("x"), lax.axis_index("c"), lax.axis_index("yl")
    z, half = lax.axis_index("z"), lax.axis_index("yh")
    way = 1 - 2 * core
    weight = value_weight[0]
    depth = weight.shape[0]
    parts = pseudo_grad[0].reshape(2, COLUMN, CORES, -1, pseudo_grad.shape[-1])

    blocks = [2 * ((z - (1 + step) * way) % RING) for step in range(RING)]
    gathered = [around(weight)]
    cotangents = (cotangent, lax.ppermute(cotangent, "yh", SWAP))
    sent, inverse = first_block((blocks[0] + 1 - half) * depth, tokens, norm_gain, depth)
    passed = copied(gathered[0], [sent])
    gathered.append(around(passed))

    starts = [(b + half) * depth for b in blocks] + [(b + 1 - half) * depth for b in blocks[1:]]
    before = [cotangents[1]]
    mine, *rest = normed_blocks(starts, (RING, 2, 3, 2), tokens, norm_gain, inverse, depth, before)
    theirs = []

    def send(sent):
        got = lax.ppermute(sent, "yh", SWAP)
        theirs.extend((got, lead(entry, got)) for entry in range(got.shape[0]))

    send(sent)
    send(rest[0])

    def products(steps, sums=(), last=False):
        return value_step(
            [(mine, lead(s, mine)) for s in steps],
            [theirs[s] for s in steps],
            [weight if s == RING - 1 else gathered[s] for s in steps],
            list(sums),
            last,
        )

    def outer_steps():
        after = yield
        got = lax.ppermute(given, "c", SWAP)
        beside = x ^ 1
        keep, give = sum_and_split(
            parts, got, ((x, 3 - x), (beside, 3 - beside)), core, BF16, [after]
        )
        got = lax.ppermute(give, "x", NEXT)
        after = yield give
        keep, give = sum_and_split(keep, got, ((0,), (1,)), None, BF16, [after])
        got = lax.ppermute(give, "x", OUTER)
        after = yield give
        keep, give = sum_and_split(keep[0], got[0], ((row,), (1 - row,)), None, F32, [after])
        got = lax.ppermute(give, "yl", SWAP)
        after = yield give
        held, new_momentum = outer_step(keep, got, fragment, outer_momentum, [after])
        got = lax.ppermute(held, "yl", SWAP)
        after = yield held
        held = join(held, got, (row, 1 - row), [after])
        got = lax.ppermute(held, "x", OUTER)
        after = yield held
        low = (x > 1).astype(jnp.int32)
        held = join(held[None], got[None], (low, 1 - low), [after])
        got = lax.ppermute(held, "x", NEXT)
        after = yield held
        ends = (x == 0) | (x == 3)
        first, second = jnp.where(ends, 0, 1), jnp.where(ends, 3, 2)
        held = join(held, got, (first, second, 1 - first, 5 - second), [after])
        got = lax.ppermute(held, "c", SWAP)
        yield held
        whole_fragment = join_cores(core, held, got)
        yield whole_fragment.reshape(-1, pseudo_grad.shape[-1]), new_momentum

    outer = outer_steps()
    next(outer)
    given = rows_of_core(parts, 1 - core, [sent])
    arrived, sums = None, ()
    for step in range(RING - 1):
        passed = gathered[step]
        if 0 < step < RING - 2:
            passed = copied(gathered[step], [total])
            gathered.append(around(passed))
        before = [passed, outer.send(mine if step == 0 else passed if step < RING - 2 else total)]
        if step in (2, 4):
            waiting = copied(rest[step // 2], [total])
            send(waiting)
            before.append(waiting)
        if step > 2:
            steps = ((0, 1), (2, 3), (4, 5), (6, 7))[step - 3]
            sums = products(steps, sums, step == RING - 2)
            before.append(sums[0])
        if step == RING - 2:
            own_gradient = gradient_step((mine, lead(RING - 1, mine)), theirs[-1], cotangents, None, F32)
            before.append(own_gradient)
        total = gradient_step(
            (mine, lead(step, mine)), theirs[step], cotangents, arrived, BF16, before
        )
        arrived = around(total)
    returned = lax.ppermute(sums[1], "yh", SWAP)
    values = (sums[0] + returned.astype(F32)).astype(BF16)
    new_fragment, new_momentum = outer.send(total)

    gradient = own_gradient + arrived.astype(F32)
    new_first = 0.9 * first_moment[0] + 0.1 * gradient
    new_second = 0.95 * second_moment[0] + 0.05 * gradient * gradient
    update = new_first / 0.6513215599 / (jnp.sqrt(new_second / 0.4012630607) + 1e-08)
    update = update + 0.1 * weight.astype(F32)
    new_weight = (weight.astype(F32) - 0.003 * update).astype(BF16)
    return (values, new_weight[None], new_first[None], new_second[None], new_fragment, new_momentum)


def solution(mesh):
    fine = Mesh(mesh.devices.reshape(2, COLUMN, CORES, RING, 2), ("yl", "x", "c", "z", "yh"))
    replica, fsdp = ("yl", "x", "c"), ("z", "yh")
    return jax.shard_map(
        body,
        mesh=fine,
        in_specs=(
            P(replica + fsdp, None),
            P(replica, None),
            P(replica + fsdp, None),
            P(replica, fsdp, None),
            P(replica, fsdp, None),
            P(replica, fsdp, None),
            P(replica, fsdp, None),
            P(fsdp + replica, None),
            P(fsdp + replica, None),
        ),
        out_specs=(
            P(replica + fsdp, None),
            P(replica, fsdp, None),
            P(replica, fsdp, None),
            P(replica, fsdp, None),
            P(fsdp, None),
            P(fsdp + replica, None),
        ),
        check_vma=False,
    )
```

```python
import jax
import jax.numpy as jnp
from jax import lax
from jax.experimental import pallas as pl
from jax.experimental.pallas import tpu as pltpu
from jax.sharding import Mesh, PartitionSpec as P

F32 = jnp.float32
BF16 = jnp.bfloat16
CORES, RING, COLUMN = 2, 8, 4
AROUND = [(z, (z + 1) % RING) for z in range(RING)] + [
    (RING + z, RING + (z - 1) % RING) for z in range(RING)
]
NEXT = [(0, 1), (1, 0), (2, 3), (3, 2)]
OUTER = [(0, 3), (3, 0), (1, 2), (2, 1)]
SWAP = [(0, 1), (1, 0)]
HINT = pl.CostEstimate(flops=2_500_000_000, bytes_accessed=12_000_000, transcendentals=0)
BRIEF = pl.CostEstimate(flops=1000, bytes_accessed=1000, transcendentals=0)


def around(value):
    return lax.ppermute(value, ("c", "z"), AROUND)


def matmul(left, right):
    return lax.dot_general(left, right, (((1,), (0,)), ((), ())), preferred_element_type=F32)


def contract_rows(left, right):
    return lax.dot_general(left, right, (((0,), (0,)), ((), ())), preferred_element_type=F32)


def whole(shape):
    return pl.BlockSpec(shape, lambda i, *_: (0,) * len(shape))


def lead(place, array):
    return pl.BlockSpec((1,) + array.shape[1:], lambda i, *_: (place,) + (0,) * (array.ndim - 1))


def tiled(shape, axis, tile):
    block = shape[:axis] + (tile,) + shape[axis + 1 :]
    return pl.BlockSpec(block, lambda i, *_: tuple(i if d == axis else 0 for d in range(len(shape))))


def turn(kernel, inputs, outs, scalars=None, steps=1, after=(), hint=HINT):
    arrays, specs = [a for a, _ in inputs], [s for _, s in inputs]
    for array in after:
        arrays.append(array)
        specs.append(whole((1,) * (array.ndim - 2) + (16, 128)))
    many = len(inputs)
    prefetched = [] if scalars is None else [jnp.stack([jnp.int32(s) for s in scalars])]

    def run(*refs):
        first = len(prefetched)
        ins, rest = refs[first : first + many], refs[first + len(arrays) :]
        kernel(refs[0] if prefetched else None, ins, rest)

    return pl.pallas_call(
        run,
        grid_spec=pltpu.PrefetchScalarGridSpec(
            num_scalar_prefetch=len(prefetched),
            grid=(steps,),
            in_specs=specs,
            out_specs=[s for _, s in outs],
        ),
        out_shape=[o for o, _ in outs],
        compiler_params=pltpu.CompilerParams(vmem_limit_bytes=16 * 2**20),
        cost_estimate=hint,
    )(*prefetched, *arrays)


def full(array):
    return array, whole(array.shape)


def new(shape, dtype):
    return jax.ShapeDtypeStruct(shape, dtype), whole(shape)


def far(array, blocks):
    return pltpu.with_memory_space_constraint(array, pltpu.HBM), blocks


def scaled(tokens_ref, gain_ref, inverse_rms, start, depth):
    at = pl.ds(pl.multiple_of(start, depth), depth)
    return (tokens_ref[:, at].astype(F32) * inverse_rms * gain_ref[:, at]).astype(BF16)


def first_block(start, tokens, norm_gain, depth):
    rows, width = tokens.shape
    tile = rows // 4

    def kernel(starts, ins, outs):
        tokens_ref, gain_ref = ins
        wide = tokens_ref[...].astype(F32)
        inverse_rms = lax.rsqrt(jnp.mean(wide * wide, axis=-1, keepdims=True) + 1e-05)
        outs[0][0] = scaled(tokens_ref, gain_ref, inverse_rms, starts[0], depth)
        outs[1][...] = jnp.broadcast_to(inverse_rms, outs[1].shape)

    block, inverse = (1, rows, depth), (rows, 128)
    return turn(
        kernel,
        [(tokens, tiled(tokens.shape, 0, tile)), full(norm_gain)],
        [
            (jax.ShapeDtypeStruct(block, BF16), tiled(block, 1, tile)),
            (jax.ShapeDtypeStruct(inverse, F32), tiled(inverse, 0, tile)),
        ],
        [start],
        4,
        hint=BRIEF,
    )


def normed_blocks(starts, sizes, tokens, norm_gain, inverse, depth, after=()):
    rows, width = tokens.shape
    tile = rows // 4

    def kernel(starts, ins, outs):
        tokens_ref, gain_ref, inverse_ref = ins
        at = 0
        for out, size in zip(outs, sizes):
            for place in range(size):
                out[place] = scaled(tokens_ref, gain_ref, inverse_ref[:, :1], starts[at], depth)
                at += 1

    shapes = [(size, rows, depth) for size in sizes]
    return turn(
        kernel,
        [
            (tokens, tiled(tokens.shape, 0, tile)),
            full(norm_gain),
            (inverse, tiled(inverse.shape, 0, tile)),
        ],
        [(pltpu.HBM(shape, BF16), tiled(shape, 1, tile)) for shape in shapes],
        starts,
        4,
        after,
    )


def copied(array, after):
    def kernel(_, ins, outs):
        outs[0][...] = ins[0][...]

    return turn(kernel, [full(array)], [new(array.shape, array.dtype)], after=after)[0]


def gradient_step(mine, theirs, cotangents, arrived, dtype, after=()):
    depth, columns = mine[0].shape[-1], cotangents[0].shape[1]
    inputs = [far(*mine), far(*theirs)] + [full(c) for c in cotangents]
    inputs += [] if arrived is None else [full(arrived)]

    def kernel(_, ins, outs):
        total = contract_rows(ins[0][0], ins[2][...]) + contract_rows(ins[1][0], ins[3][...])
        if arrived is not None:
            total = total + ins[4][...].astype(F32)
        outs[0][...] = total.astype(dtype)

    return turn(kernel, inputs, [new((depth, columns), dtype)], after=after)[0]


def value_step(mine, theirs, weights, sums, last=False, after=()):
    many = len(weights)
    rows, columns = mine[0][0].shape[1], weights[0].shape[1]
    inputs = [far(*m) for m in mine] + [far(*t) for t in theirs] + [full(w) for w in weights] + [full(s) for s in sums]

    def kernel(_, ins, outs):
        for side in range(2):
            value = sum(matmul(ins[side * many + p][0], ins[2 * many + p][...]) for p in range(many))
            if sums:
                value = value + ins[3 * many + side][...]
            outs[side][...] = value.astype(outs[side].dtype)

    shape = (rows, columns)
    return turn(kernel, inputs, [new(shape, F32), new(shape, BF16 if last else F32)], after=after)


def rows_of_core(parts, core, after):
    lines, columns, _, rows, width = parts.shape

    def kernel(_, ins, outs):
        outs[0][...] = ins[0][:, :, 0].swapaxes(0, 1)

    block = pl.BlockSpec((lines, columns, 1, rows, width), lambda i, core: (0, 0, core[0], 0, 0))
    return turn(kernel, [(parts, block)], [new((columns, lines, rows, width), BF16)], [core], 1, after, BRIEF)[0]


def sum_and_split(mine, got, picks, core=None, first=BF16, after=()):
    shape = got.shape
    sizes = [len(group) for group in picks]
    places = [p for group in picks for p in group]
    spec = whole(mine.shape)
    if core is not None:
        lines, columns, _, rows, width = mine.shape
        last = len(places)
        places.append(core)
        spec = pl.BlockSpec((lines, columns, 1, rows, width), lambda i, s: (0, 0, s[last], 0, 0))

    def kernel(places, ins, outs):
        at = 0
        for out, size in zip(outs, sizes):
            for place in range(size):
                index = places[at]
                held = ins[0][index] if core is None else ins[0][:, index, 0]
                out[place] = (held.astype(F32) + ins[1][index].astype(F32)).astype(out.dtype)
                at += 1

    outs = [new((size,) + shape[1:], first if out == 0 else BF16) for out, size in enumerate(sizes)]
    return turn(kernel, [(mine, spec), full(got)], outs, places, 1, after)


def outer_step(mine, got, fragment, momentum, after):
    def kernel(_, ins, outs):
        average = (ins[0][0] + ins[1][0].astype(F32)) / 16
        moved = 0.9 * ins[3][...] + average
        outs[0][0] = (ins[2][...] - 0.7 * (average + 0.9 * moved)).astype(BF16)
        outs[1][...] = moved

    shape = fragment.shape
    return turn(
        kernel,
        [full(mine), full(got), full(fragment), full(momentum)],
        [new((1,) + shape, BF16), new(shape, F32)],
        after=after,
    )


def join(mine, got, places, after=()):
    many = mine.shape[0]

    def kernel(places, ins, outs):
        for side in range(2):
            for place in range(many):
                outs[0][places[side * many + place]] = ins[side][place]

    return turn(kernel, [full(mine), full(got)], [new((2 * many,) + mine.shape[1:], BF16)], places, 1, after)[0]


def join_cores(core, mine, got):
    columns, lines, rows, width = mine.shape

    def kernel(core, ins, outs):
        for line in range(lines):
            for column in range(columns):
                outs[0][line, column, core[0]] = ins[0][column, line]
                outs[0][line, column, 1 - core[0]] = ins[1][column, line]

    return turn(kernel, [full(mine), full(got)], [new((lines, columns, CORES, rows, width), BF16)], [core])[0]


def body(
    tokens,
    norm_gain,
    cotangent,
    value_weight,
    first_moment,
    second_moment,
    pseudo_grad,
    fragment,
    outer_momentum,
):
    x, core, row = lax.axis_index("x"), lax.axis_index("c"), lax.axis_index("yl")
    z, half = lax.axis_index("z"), lax.axis_index("yh")
    way = 1 - 2 * core
    weight = value_weight[0]
    depth = weight.shape[0]
    parts = pseudo_grad[0].reshape(2, COLUMN, CORES, -1, pseudo_grad.shape[-1])

    blocks = [2 * ((z - (1 + step) * way) % RING) for step in range(RING)]
    gathered = [around(weight)]
    cotangents = (cotangent, lax.ppermute(cotangent, "yh", SWAP))
    sent, inverse = first_block((blocks[0] + 1 - half) * depth, tokens, norm_gain, depth)
    passed = copied(gathered[0], [sent])
    gathered.append(around(passed))

    starts = [(b + half) * depth for b in blocks] + [(b + 1 - half) * depth for b in blocks[1:]]
    before = [cotangents[1]]
    mine, *rest = normed_blocks(starts, (RING, 2, 3, 2), tokens, norm_gain, inverse, depth, before)
    theirs = []

    def send(sent):
        got = lax.ppermute(sent, "yh", SWAP)
        theirs.extend((got, lead(entry, got)) for entry in range(got.shape[0]))

    send(sent)
    send(rest[0])

    def products(steps, sums=(), last=False):
        return value_step(
            [(mine, lead(s, mine)) for s in steps],
            [theirs[s] for s in steps],
            [weight if s == RING - 1 else gathered[s] for s in steps],
            list(sums),
            last,
        )

    def outer_steps():
        after = yield
        got = lax.ppermute(given, "c", SWAP)
        beside = x ^ 1
        keep, give = sum_and_split(
            parts, got, ((x, 3 - x), (beside, 3 - beside)), core, BF16, [after]
        )
        got = lax.ppermute(give, "x", NEXT)
        after = yield give
        keep, give = sum_and_split(keep, got, ((0,), (1,)), None, BF16, [after])
        got = lax.ppermute(give, "x", OUTER)
        after = yield give
        keep, give = sum_and_split(keep[0], got[0], ((row,), (1 - row,)), None, F32, [after])
        got = lax.ppermute(give, "yl", SWAP)
        after = yield give
        held, new_momentum = outer_step(keep, got, fragment, outer_momentum, [after])
        got = lax.ppermute(held, "yl", SWAP)
        after = yield held
        held = join(held, got, (row, 1 - row), [after])
        got = lax.ppermute(held, "x", OUTER)
        after = yield held
        low = (x > 1).astype(jnp.int32)
        held = join(held[None], got[None], (low, 1 - low), [after])
        got = lax.ppermute(held, "x", NEXT)
        after = yield held
        ends = (x == 0) | (x == 3)
        first, second = jnp.where(ends, 0, 1), jnp.where(ends, 3, 2)
        held = join(held, got, (first, second, 1 - first, 5 - second), [after])
        got = lax.ppermute(held, "c", SWAP)
        yield held
        whole_fragment = join_cores(core, held, got)
        yield whole_fragment.reshape(-1, pseudo_grad.shape[-1]), new_momentum

    outer = outer_steps()
    next(outer)
    given = rows_of_core(parts, 1 - core, [sent])
    arrived, sums = None, ()
    for step in range(RING - 1):
        passed = gathered[step]
        if 0 < step < RING - 2:
            passed = copied(gathered[step], [total])
            gathered.append(around(passed))
        before = [passed, outer.send(mine if step == 0 else passed if step < RING - 2 else total)]
        if step in (2, 4):
            waiting = copied(rest[step // 2], [total])
            send(waiting)
            before.append(waiting)
        if step > 2:
            steps = ((0, 1), (2, 3), (4, 5), (6, 7))[step - 3]
            sums = products(steps, sums, step == RING - 2)
            before.append(sums[0])
        if step == RING - 2:
            own_gradient = gradient_step((mine, lead(RING - 1, mine)), theirs[-1], cotangents, None, F32)
            before.append(own_gradient)
        total = gradient_step(
            (mine, lead(step, mine)), theirs[step], cotangents, arrived, BF16, before
        )
        arrived = around(total)
    returned = lax.ppermute(sums[1], "yh", SWAP)
    values = (sums[0] + returned.astype(F32)).astype(BF16)
    new_fragment, new_momentum = outer.send(total)

    gradient = own_gradient + arrived.astype(F32)
    new_first = 0.9 * first_moment[0] + 0.1 * gradient
    new_second = 0.95 * second_moment[0] + 0.05 * gradient * gradient
    update = new_first / 0.6513215599 / (jnp.sqrt(new_second / 0.4012630607) + 1e-08)
    update = update + 0.1 * weight.astype(F32)
    new_weight = (weight.astype(F32) - 0.003 * update).astype(BF16)
    return (values, new_weight[None], new_first[None], new_second[None], new_fragment, new_momentum)


def solution(mesh):
    fine = Mesh(mesh.devices.reshape(2, COLUMN, CORES, RING, 2), ("yl", "x", "c", "z", "yh"))
    replica, fsdp = ("yl", "x", "c"), ("z", "yh")
    return jax.shard_map(
        body,
        mesh=fine,
        in_specs=(
            P(replica + fsdp, None),
            P(replica, None),
            P(replica + fsdp, None),
            P(replica, fsdp, None),
            P(replica, fsdp, None),
            P(replica, fsdp, None),
            P(replica, fsdp, None),
            P(fsdp + replica, None),
            P(fsdp + replica, None),
        ),
        out_specs=(
            P(replica + fsdp, None),
            P(replica, fsdp, None),
            P(replica, fsdp, None),
            P(replica, fsdp, None),
            P(fsdp, None),
            P(fsdp + replica, None),
        ),
        check_vma=False,
    )
```

```python
import jax
import jax.numpy as jnp
from jax import lax
from jax.experimental import pallas as pl
from jax.experimental.pallas import tpu as pltpu
from jax.sharding import Mesh, PartitionSpec as P

F32 = jnp.float32
BF16 = jnp.bfloat16
CORES, RING, COLUMN = 2, 8, 4
AROUND = [(z, (z + 1) % RING) for z in range(RING)] + [
    (RING + z, RING + (z - 1) % RING) for z in range(RING)
]
NEXT = [(0, 1), (1, 0), (2, 3), (3, 2)]
OUTER = [(0, 3), (3, 0), (1, 2), (2, 1)]
SWAP = [(0, 1), (1, 0)]
HINT = pl.CostEstimate(flops=2_500_000_000, bytes_accessed=12_000_000, transcendentals=0)
BRIEF = pl.CostEstimate(flops=1000, bytes_accessed=1000, transcendentals=0)


def around(value):
    return lax.ppermute(value, ("c", "z"), AROUND)


def matmul(left, right):
    return lax.dot_general(left, right, (((1,), (0,)), ((), ())), preferred_element_type=F32)


def contract_rows(left, right):
    return lax.dot_general(left, right, (((0,), (0,)), ((), ())), preferred_element_type=F32)


def whole(shape):
    return pl.BlockSpec(shape, lambda i, *_: (0,) * len(shape))


def lead(place, array):
    return pl.BlockSpec((1,) + array.shape[1:], lambda i, *_: (place,) + (0,) * (array.ndim - 1))


def tiled(shape, axis, tile):
    block = shape[:axis] + (tile,) + shape[axis + 1 :]
    return pl.BlockSpec(block, lambda i, *_: tuple(i if d == axis else 0 for d in range(len(shape))))


def turn(kernel, inputs, outs, scalars=None, steps=1, after=(), hint=HINT):
    arrays, specs = [a for a, _ in inputs], [s for _, s in inputs]
    for array in after:
        arrays.append(array)
        specs.append(whole((1,) * (array.ndim - 2) + (16, 128)))
    many = len(inputs)
    prefetched = [] if scalars is None else [jnp.stack([jnp.int32(s) for s in scalars])]

    def run(*refs):
        first = len(prefetched)
        ins, rest = refs[first : first + many], refs[first + len(arrays) :]
        kernel(refs[0] if prefetched else None, ins, rest)

    return pl.pallas_call(
        run,
        grid_spec=pltpu.PrefetchScalarGridSpec(
            num_scalar_prefetch=len(prefetched),
            grid=(steps,),
            in_specs=specs,
            out_specs=[s for _, s in outs],
        ),
        out_shape=[o for o, _ in outs],
        compiler_params=pltpu.CompilerParams(vmem_limit_bytes=16 * 2**20),
        cost_estimate=hint,
    )(*prefetched, *arrays)


def full(array):
    return array, whole(array.shape)


def new(shape, dtype):
    return jax.ShapeDtypeStruct(shape, dtype), whole(shape)


def far(array, blocks):
    return pltpu.with_memory_space_constraint(array, pltpu.HBM), blocks


def scaled(tokens_ref, gain_ref, inverse_rms, start, depth):
    at = pl.ds(pl.multiple_of(start, depth), depth)
    return (tokens_ref[:, at].astype(F32) * inverse_rms * gain_ref[:, at]).astype(BF16)


def first_block(start, tokens, norm_gain, depth):
    rows, width = tokens.shape
    tile = rows // 4

    def kernel(starts, ins, outs):
        tokens_ref, gain_ref = ins
        wide = tokens_ref[...].astype(F32)
        inverse_rms = lax.rsqrt(jnp.mean(wide * wide, axis=-1, keepdims=True) + 1e-05)
        outs[0][0] = scaled(tokens_ref, gain_ref, inverse_rms, starts[0], depth)
        outs[1][...] = jnp.broadcast_to(inverse_rms, outs[1].shape)

    block, inverse = (1, rows, depth), (rows, 128)
    return turn(
        kernel,
        [(tokens, tiled(tokens.shape, 0, tile)), full(norm_gain)],
        [
            (jax.ShapeDtypeStruct(block, BF16), tiled(block, 1, tile)),
            (jax.ShapeDtypeStruct(inverse, F32), tiled(inverse, 0, tile)),
        ],
        [start],
        4,
        hint=BRIEF,
    )


def normed_blocks(starts, sizes, tokens, norm_gain, inverse, depth, after=()):
    rows, width = tokens.shape
    tile = rows // 4

    def kernel(starts, ins, outs):
        tokens_ref, gain_ref, inverse_ref = ins
        at = 0
        for out, size in zip(outs, sizes):
            for place in range(size):
                out[place] = scaled(tokens_ref, gain_ref, inverse_ref[:, :1], starts[at], depth)
                at += 1

    shapes = [(size, rows, depth) for size in sizes]
    return turn(
        kernel,
        [
            (tokens, tiled(tokens.shape, 0, tile)),
            full(norm_gain),
            (inverse, tiled(inverse.shape, 0, tile)),
        ],
        [(pltpu.HBM(shape, BF16), tiled(shape, 1, tile)) for shape in shapes],
        starts,
        4,
        after,
    )


def copied(array, after):
    def kernel(_, ins, outs):
        outs[0][...] = ins[0][...]

    return turn(kernel, [full(array)], [new(array.shape, array.dtype)], after=after)[0]


def gradient_step(mine, theirs, cotangents, arrived, dtype, after=()):
    depth, columns = mine[0].shape[-1], cotangents[0].shape[1]
    inputs = [far(*mine), far(*theirs)] + [full(c) for c in cotangents]
    inputs += [] if arrived is None else [full(arrived)]

    def kernel(_, ins, outs):
        total = contract_rows(ins[0][0], ins[2][...]) + contract_rows(ins[1][0], ins[3][...])
        if arrived is not None:
            total = total + ins[4][...].astype(F32)
        outs[0][...] = total.astype(dtype)

    return turn(kernel, inputs, [new((depth, columns), dtype)], after=after)[0]


def value_step(mine, theirs, weights, sums, last=False, after=()):
    many = len(weights)
    rows, columns = mine[0][0].shape[1], weights[0].shape[1]
    inputs = [far(*m) for m in mine] + [far(*t) for t in theirs] + [full(w) for w in weights] + [full(s) for s in sums]

    def kernel(_, ins, outs):
        for side in range(2):
            value = sum(matmul(ins[side * many + p][0], ins[2 * many + p][...]) for p in range(many))
            if sums:
                value = value + ins[3 * many + side][...]
            outs[side][...] = value.astype(outs[side].dtype)

    shape = (rows, columns)
    return turn(kernel, inputs, [new(shape, F32), new(shape, BF16 if last else F32)], after=after)


def rows_of_core(parts, core, after):
    lines, columns, _, rows, width = parts.shape

    def kernel(_, ins, outs):
        outs[0][...] = ins[0][:, :, 0].swapaxes(0, 1)

    block = pl.BlockSpec((lines, columns, 1, rows, width), lambda i, core: (0, 0, core[0], 0, 0))
    return turn(kernel, [(parts, block)], [new((columns, lines, rows, width), BF16)], [core], 1, after, BRIEF)[0]


def sum_and_split(mine, got, picks, core=None, first=BF16, after=()):
    shape = got.shape
    sizes = [len(group) for group in picks]
    places = [p for group in picks for p in group]
    spec = whole(mine.shape)
    if core is not None:
        lines, columns, _, rows, width = mine.shape
        last = len(places)
        places.append(core)
        spec = pl.BlockSpec((lines, columns, 1, rows, width), lambda i, s: (0, 0, s[last], 0, 0))

    def kernel(places, ins, outs):
        at = 0
        for out, size in zip(outs, sizes):
            for place in range(size):
                index = places[at]
                held = ins[0][index] if core is None else ins[0][:, index, 0]
                out[place] = (held.astype(F32) + ins[1][index].astype(F32)).astype(out.dtype)
                at += 1

    outs = [new((size,) + shape[1:], first if out == 0 else BF16) for out, size in enumerate(sizes)]
    return turn(kernel, [(mine, spec), full(got)], outs, places, 1, after)


def outer_step(mine, got, fragment, momentum, after):
    def kernel(_, ins, outs):
        average = (ins[0][0] + ins[1][0].astype(F32)) / 16
        moved = 0.9 * ins[3][...] + average
        outs[0][0] = (ins[2][...] - 0.7 * (average + 0.9 * moved)).astype(BF16)
        outs[1][...] = moved

    shape = fragment.shape
    return turn(
        kernel,
        [full(mine), full(got), full(fragment), full(momentum)],
        [new((1,) + shape, BF16), new(shape, F32)],
        after=after,
    )


def join(mine, got, places, after=()):
    many = mine.shape[0]

    def kernel(places, ins, outs):
        for side in range(2):
            for place in range(many):
                outs[0][places[side * many + place]] = ins[side][place]

    return turn(kernel, [full(mine), full(got)], [new((2 * many,) + mine.shape[1:], BF16)], places, 1, after)[0]


def join_cores(core, mine, got):
    columns, lines, rows, width = mine.shape

    def kernel(core, ins, outs):
        for line in range(lines):
            for column in range(columns):
                outs[0][line, column, core[0]] = ins[0][column, line]
                outs[0][line, column, 1 - core[0]] = ins[1][column, line]

    return turn(kernel, [full(mine), full(got)], [new((lines, columns, CORES, rows, width), BF16)], [core])[0]


def body(
    tokens,
    norm_gain,
    cotangent,
    value_weight,
    first_moment,
    second_moment,
    pseudo_grad,
    fragment,
    outer_momentum,
):
    x, core, row = lax.axis_index("x"), lax.axis_index("c"), lax.axis_index("yl")
    z, half = lax.axis_index("z"), lax.axis_index("yh")
    way = 1 - 2 * core
    weight = value_weight[0]
    depth = weight.shape[0]
    parts = pseudo_grad[0].reshape(2, COLUMN, CORES, -1, pseudo_grad.shape[-1])

    blocks = [2 * ((z - (1 + step) * way) % RING) for step in range(RING)]
    gathered = [around(weight)]
    cotangents = (cotangent, lax.ppermute(cotangent, "yh", SWAP))
    sent, inverse = first_block((blocks[0] + 1 - half) * depth, tokens, norm_gain, depth)
    passed = copied(gathered[0], [sent])
    gathered.append(around(passed))

    starts = [(b + half) * depth for b in blocks] + [(b + 1 - half) * depth for b in blocks[1:]]
    before = [cotangents[1]]
    mine, *rest = normed_blocks(starts, (RING, 2, 3, 2), tokens, norm_gain, inverse, depth, before)
    theirs = []

    def send(sent):
        got = lax.ppermute(sent, "yh", SWAP)
        theirs.extend((got, lead(entry, got)) for entry in range(got.shape[0]))

    send(sent)
    send(rest[0])

    def products(steps, sums=(), last=False):
        return value_step(
            [(mine, lead(s, mine)) for s in steps],
            [theirs[s] for s in steps],
            [weight if s == RING - 1 else gathered[s] for s in steps],
            list(sums),
            last,
        )

    def outer_steps():
        after = yield
        got = lax.ppermute(given, "c", SWAP)
        beside = x ^ 1
        keep, give = sum_and_split(
            parts, got, ((x, 3 - x), (beside, 3 - beside)), core, BF16, [after]
        )
        got = lax.ppermute(give, "x", NEXT)
        after = yield give
        keep, give = sum_and_split(keep, got, ((0,), (1,)), None, BF16, [after])
        got = lax.ppermute(give, "x", OUTER)
        after = yield give
        keep, give = sum_and_split(keep[0], got[0], ((row,), (1 - row,)), None, F32, [after])
        got = lax.ppermute(give, "yl", SWAP)
        after = yield give
        held, new_momentum = outer_step(keep, got, fragment, outer_momentum, [after])
        got = lax.ppermute(held, "yl", SWAP)
        after = yield held
        held = join(held, got, (row, 1 - row), [after])
        got = lax.ppermute(held, "x", OUTER)
        after = yield held
        low = (x > 1).astype(jnp.int32)
        held = join(held[None], got[None], (low, 1 - low), [after])
        got = lax.ppermute(held, "x", NEXT)
        after = yield held
        ends = (x == 0) | (x == 3)
        first, second = jnp.where(ends, 0, 1), jnp.where(ends, 3, 2)
        held = join(held, got, (first, second, 1 - first, 5 - second), [after])
        got = lax.ppermute(held, "c", SWAP)
        yield held
        whole_fragment = join_cores(core, held, got)
        yield whole_fragment.reshape(-1, pseudo_grad.shape[-1]), new_momentum

    outer = outer_steps()
    next(outer)
    given = rows_of_core(parts, 1 - core, [sent])
    arrived, sums, turns = None, (), []
    for step in range(RING - 1):
        passed = gathered[step]
        if 0 < step < RING - 2:
            passed = copied(gathered[step], [total])
            gathered.append(around(passed))
        before = [passed]
        turned = outer.send(mine if step == 0 else passed if step < RING - 2 else total)
        turns.append(turned)
        before += {2: turns[1:2], 3: turns[2:3], 4: turns[3:5], 5: turns[5:], 6: turns[6:]}.get(step, [])
        if step in (2, 4):
            waiting = copied(rest[step // 2], [total])
            send(waiting)
            before.append(waiting)
        if step > 2:
            steps = ((0, 1), (2, 3), (4, 5), (6, 7))[step - 3]
            sums = products(steps, sums, step == RING - 2)
            before.append(sums[0])
        if step == RING - 2:
            own_gradient = gradient_step((mine, lead(RING - 1, mine)), theirs[-1], cotangents, None, F32)
            before.append(own_gradient)
        total = gradient_step(
            (mine, lead(step, mine)), theirs[step], cotangents, arrived, BF16, before
        )
        arrived = around(total)
    returned = lax.ppermute(sums[1], "yh", SWAP)
    values = (sums[0] + returned.astype(F32)).astype(BF16)
    new_fragment, new_momentum = outer.send(total)

    gradient = own_gradient + arrived.astype(F32)
    new_first = 0.9 * first_moment[0] + 0.1 * gradient
    new_second = 0.95 * second_moment[0] + 0.05 * gradient * gradient
    update = new_first / 0.6513215599 / (jnp.sqrt(new_second / 0.4012630607) + 1e-08)
    update = update + 0.1 * weight.astype(F32)
    new_weight = (weight.astype(F32) - 0.003 * update).astype(BF16)
    return (values, new_weight[None], new_first[None], new_second[None], new_fragment, new_momentum)


def solution(mesh):
    fine = Mesh(mesh.devices.reshape(2, COLUMN, CORES, RING, 2), ("yl", "x", "c", "z", "yh"))
    replica, fsdp = ("yl", "x", "c"), ("z", "yh")
    return jax.shard_map(
        body,
        mesh=fine,
        in_specs=(
            P(replica + fsdp, None),
            P(replica, None),
            P(replica + fsdp, None),
            P(replica, fsdp, None),
            P(replica, fsdp, None),
            P(replica, fsdp, None),
            P(replica, fsdp, None),
            P(fsdp + replica, None),
            P(fsdp + replica, None),
        ),
        out_specs=(
            P(replica + fsdp, None),
            P(replica, fsdp, None),
            P(replica, fsdp, None),
            P(replica, fsdp, None),
            P(fsdp, None),
            P(fsdp + replica, None),
        ),
        check_vma=False,
    )
```
